32 devices in a mesh: offset: 2 (over x), inline: 4 (over z), tm: 4 (over y, core).
Axes of the slice: x: 2, y: 2, z: 4, core: 2. Of those that a mesh axis runs over, the one named last changes fastest.
Arguments:
- traces: float32 [2, 32, 16, 2048], P('offset', 'inline', None, 'tm'), may hold values from -6 to 6
- class_of_block: int32 [2], P('offset'), may hold values from 0 to 15, as said below
- band_start: int32 [16, 5, 2048], P(None, None, 'tm'), may hold values from 0 to 121
- band_weights: float32 [16, 5, 8, 2048], P(None, None, None, 'tm'), may hold values from -1 to 1
Outputs:
- migrated: float32 [32, 16, 2048], P('inline', None, 'tm')
- residual: float32 [2, 32, 16, 2048], P('offset', 'inline', None, 'tm')
The draws below stay inside these ranges and needn't reach their ends.
Inputs may be any that keep to these rules, and one draw needn't show every extreme that they name: band_start[c, a, t] is the smallest delay of the band that data time t reads from the image at aperture distance a - 2; the band's delays are band_start[c, a, t] + k for k below 8. `class_of_block`: the first min(2, 16) blocks have different classes, and class 16 - 1 is among them.
All inputs are finite; a program needn't handle non-finite values.
Results may differ from the reference program's by a relative error of at most 0.0003.
Values sent between devices are 32-bit elements; how exact they have to be, the bound alone decides.
A program may use at most 64 MiB of HBM per device.

```python
import jax
import jax.numpy as jnp
from jax import lax

NT = 2048
NCLASS = 16
K = 8
LAG = 128
APER = 2
ITERS = 2
XL = 16
NI = 32
BLOCKS = 2


def draw_class_of_block(key, part):
    key = jax.random.fold_in(key, 11)
    first_key = jax.random.fold_in(key, 1)
    second_key = jax.random.fold_in(key, 2)
    third_key = jax.random.fold_in(key, 3)
    leading = min(BLOCKS, NCLASS)
    shuffled = jax.random.permutation(first_key, jnp.arange(NCLASS, dtype=jnp.int32))
    chosen = jax.random.randint(third_key, (), 0, leading, dtype=jnp.int32)
    rotation = (NCLASS - 1 - shuffled[chosen]).astype(jnp.int32)
    shuffled = ((shuffled + rotation) % NCLASS).astype(jnp.int32)
    block_ids = jnp.arange(BLOCKS, dtype=jnp.int32)
    random_classes = jax.random.randint(second_key, (BLOCKS,), 0, NCLASS, dtype=jnp.int32)
    return jnp.where(block_ids < NCLASS, shuffled[block_ids % NCLASS], random_classes).astype(jnp.int32)


def plant(drawn, stream_key, least, top_value):
    longest = drawn.shape.index(max(drawn.shape))
    spots = []
    for shift in (0, 1):
        where = [jax.random.randint(jax.random.fold_in(stream_key, axis), (), 0, length) for axis, length in enumerate(drawn.shape)]
        where[longest] = (where[longest] + shift) % drawn.shape[longest]
        spots.append(tuple(where))
    return drawn.at[spots[0]].set(least).at[spots[1]].set(top_value)


def steps_of(stream_key, shape, split, least, top_value):
    def one(dim, parts):
        steps = jax.random.uniform(jax.random.fold_in(jax.random.fold_in(stream_key, 6), dim), (parts,), jnp.float32, least / len(split), top_value / len(split))
        return jnp.repeat(jnp.exp(steps), shape[dim] // parts).reshape((-1,) + (1,) * (len(shape) - dim - 1))

    level = one(*split[0])
    for cut in split[1:]:
        level = level * one(*cut)
    return level


def noise(rng, shape, deviation, most, shards=(), held_as=jnp.bfloat16):
    entries = deviation * jax.random.normal(rng, shape, jnp.float32)
    if shards:
        entries = entries * steps_of(rng, shape, shards, -0.22, 0.18)
    return jnp.clip(entries, -most, most).astype(held_as)


def setup_inputs(seed: int = 0) -> dict:
    splits = jax.random.split(jax.random.key(seed), 5)
    return {
        "traces": noise(splits[0], (BLOCKS, NI, XL, NT), 1.0, 6.0, ((0, 2), (1, 4), (3, 4)), jnp.float32),
        "class_of_block": draw_class_of_block(jax.random.fold_in(splits[4], 71), 0),
        "band_start": plant(jax.random.randint(splits[2], (NCLASS, 2 * APER + 1, NT), 0, LAG - K + 2), jax.random.fold_in(splits[2], 1), 0, (LAG - K + 2) - 1).astype(jnp.int32),
        "band_weights": noise(splits[3], (NCLASS, 2 * APER + 1, K, NT), ((2 * APER + 1) * K) ** -0.5, 1.0, ((3, 4),), jnp.float32),
    }


def demigrate_block(image_field, weights, starts):
    padded = jnp.pad(image_field, ((APER, APER), (0, 0), (LAG, 0)))
    sample_rows = jnp.arange(NT, dtype=jnp.int32)
    result_sum = jnp.zeros(image_field.shape, jnp.float32)
    for aper_index in range(2 * APER + 1):
        inline_rows = padded[aper_index:aper_index + NI]
        for tap_index in range(K):
            source = (sample_rows - starts[aper_index] - tap_index + LAG).astype(jnp.int32)
            result_sum = result_sum + weights[aper_index, tap_index] * jnp.take(inline_rows, source, axis=2)
    return result_sum

def reference(traces, class_of_block, band_start, band_weights):

    def demigrate(image_field):

        def one_block(block_index):
            chosen = class_of_block[block_index]
            return demigrate_block(image_field, band_weights[chosen], band_start[chosen])
        return lax.map(one_block, jnp.arange(BLOCKS, dtype=jnp.int32))
    blank = jnp.zeros((NI, XL, NT), jnp.float32)
    unused, adjoint_fn = jax.vjp(demigrate, blank)

    def migrate(values):
        return adjoint_fn(values)[0]
    migrated = blank
    residual = traces
    gradient = migrate(residual)
    direction = gradient
    grad_norm = jnp.sum(gradient * gradient)
    for iteration in range(ITERS):
        projected = demigrate(direction)
        curvature = jnp.sum(projected * projected)
        step_size = grad_norm / curvature
        migrated = migrated + step_size * direction
        residual = residual - step_size * projected
        if iteration + 1 < ITERS:
            gradient = migrate(residual)
            grad_new = jnp.sum(gradient * gradient)
            direction = gradient + grad_new / grad_norm * direction
            grad_norm = grad_new
    return (migrated, residual)
```

```python
import functools

import jax
import jax.numpy as jnp
from jax import lax
from jax.experimental import pallas as pl
from jax.experimental.pallas import tpu as pltpu
from jax.sharding import PartitionSpec as P

K = 8
LAG = 128
APER = 2
ITERS = 2


def with_halo(block, sides, width):
    for axis, dim in sides:
        count = lax.axis_size(axis)
        forward = [(i, i + 1) for i in range(count - 1)]
        backward = [(target, source) for source, target in forward]
        low = lax.ppermute(
            lax.slice_in_dim(block, block.shape[dim] - width, None, axis=dim), axis, forward
        )
        high = lax.ppermute(lax.slice_in_dim(block, 0, width, axis=dim), axis, backward)
        block = jnp.concatenate([low, block, high], axis=dim)
    return block


def shifted(shard, axis, by):
    count = lax.axis_size(axis)
    pairs = [(i, i + by) for i in range(count) if 0 <= i + by < count]
    return lax.ppermute(shard, axis, pairs)


def widen_inline(field):
    return with_halo(field, (("inline", 1),), APER)


def totalled(value):
    return lax.psum(value, ("offset", "inline", "tm"))


def on_device_general(traces, class_of_block, band_start, band_weights):
    own_class = class_of_block[0]
    weights = lax.dynamic_index_in_dim(band_weights, own_class, 0, keepdims=False)
    starts = lax.dynamic_index_in_dim(band_start, own_class, 0, keepdims=False)
    inlines = traces.shape[1]
    crosslines = traces.shape[2]
    window = traces.shape[3]
    flat_rows = inlines * crosslines
    sample_rows = jnp.arange(window, dtype=jnp.int32)[:, None]
    sample_cols = jnp.arange(window + LAG, dtype=jnp.int32)[None, :]
    band_list = []
    for aper_index in range(2 * APER + 1):
        band_matrix = jnp.zeros((window, window + LAG), jnp.float32)
        for tap_index in range(K):
            target = sample_rows - starts[aper_index][:, None] - tap_index + LAG
            band_matrix = band_matrix + jnp.where(
                sample_cols == target, weights[aper_index, tap_index][:, None], 0.0
            )
        band_list.append(band_matrix)

    def migrate_block(values):
        widened = widen_inline(values)[0]
        result_sum = jnp.zeros((flat_rows, window + LAG), jnp.float32)
        for aper_index in range(2 * APER + 1):
            first = 2 * APER - aper_index
            slab_rows = widened[first : first + inlines].reshape(flat_rows, window)
            result_sum = result_sum + jnp.dot(
                slab_rows,
                band_list[aper_index],
                precision=lax.Precision.HIGHEST,
                preferred_element_type=jnp.float32,
            )
        result_sum = result_sum.reshape(inlines, crosslines, window + LAG)
        later_part = shifted(result_sum[:, :, :LAG], "tm", -1)
        own_part = result_sum[:, :, LAG:]
        return own_part.at[:, :, window - LAG :].add(later_part)

    def migrate(values):
        partial_image = migrate_block(values)
        gradient = lax.psum(partial_image, "offset")
        grad_norm = totalled(jnp.sum(gradient * gradient)) / lax.axis_size("offset")
        return (gradient, grad_norm)

    migrated = jnp.zeros((inlines, crosslines, window), jnp.float32)
    residual = traces
    gradient, grad_norm = migrate(residual)
    direction = gradient
    for iteration in range(ITERS):
        demigrate_widened = widen_inline(direction[None])[0]
        earlier = shifted(demigrate_widened[:, :, window - LAG :], "tm", 1)
        full_block = jnp.concatenate([earlier, demigrate_widened], axis=2)
        demigrate_result_sum = jnp.zeros((flat_rows, window), jnp.float32)
        for demigrate_aper_index in range(2 * APER + 1):
            demigrate_slab_rows = full_block[
                demigrate_aper_index : demigrate_aper_index + inlines
            ].reshape(flat_rows, window + LAG)
            demigrate_result_sum = demigrate_result_sum + lax.dot_general(
                demigrate_slab_rows,
                band_list[demigrate_aper_index],
                (((1,), (1,)), ((), ())),
                precision=lax.Precision.HIGHEST,
                preferred_element_type=jnp.float32,
            )
        projected = demigrate_result_sum.reshape(1, inlines, crosslines, window)
        curvature = totalled(jnp.sum(projected * projected))
        step_size = grad_norm / curvature
        migrated = migrated + step_size * direction
        residual = residual - step_size * projected
        if iteration + 1 < ITERS:
            gradient, grad_new = migrate(residual)
            direction = gradient + grad_new / grad_norm * direction
            grad_norm = grad_new
    return (migrated, residual)


TB = 128
MESH = pl.DeviceIdType.MESH
NAPER = 2 * APER + 1


def kernel(
    n_in, n_tm,
    cls_ref, tr_ref, st_ref, w_ref, mig_ref, res_ref,
    vt, p0, p1, ext, prev_strip, next_strip, img, bh, bl, cl, sa, sb, mg, px,
    local_sem, send_sem, recv_sem,
):
    o = lax.axis_index("offset")
    i = lax.axis_index("inline")
    t = lax.axis_index("tm")
    other = 1 - o
    rows, window = tr_ref.shape[1], tr_ref.shape[3]
    xl = tr_ref.shape[2] // 2
    tiles = window // TB
    flat = rows * xl
    own_x = pl.ds(pl.multiple_of(o * xl, xl), xl)
    other_x = pl.ds(pl.multiple_of(other * xl, xl), xl)
    plane = 2 * n_tm
    m = o * n_tm + t

    barrier = pltpu.get_barrier_semaphore()
    greeted = []
    for d in range(1, plane):
        peer = lax.rem(m + d, plane)
        greeted.append((lax.div(peer, n_tm), i, lax.rem(peer, n_tm)))
    for d in range(1, n_in):
        greeted.append((o, lax.rem(i + d, n_in), t))
    for di in sorted({1 % n_in, n_in - 1} - {0}):
        greeted.append((other, lax.rem(i + di, n_in), t))
        for dt in sorted({1 % n_tm, n_tm - 1} - {0}):
            greeted.append((o, lax.rem(i + di, n_in), lax.rem(t + dt, n_tm)))
    for device in greeted:
        pl.semaphore_signal(barrier, inc=1, device_id=device, device_id_type=MESH)
    pl.semaphore_wait(barrier, len(greeted))

    used = [0]

    def both(first, second):
        if first is None:
            return second
        if second is None:
            return first
        return jnp.logical_and(first, second)

    def inside(index, step, count):
        if step == 0:
            return None
        if step > 0:
            return index + step < count
        return index + step >= 0

    def guarded(condition, action):
        if condition is None:
            action()
        else:
            pl.when(condition)(action)

    class Message:
        def __init__(self, src, dst, device, can_send=None, can_receive=None):
            number = used[0]
            used[0] += 1
            self.copy = pltpu.make_async_remote_copy(
                src_ref=src, dst_ref=dst,
                send_sem=send_sem.at[number], recv_sem=recv_sem.at[number],
                device_id=device, device_id_type=MESH,
            )
            self.can_send, self.can_receive = can_send, can_receive
            guarded(can_send, self.copy.start)

        def received(self):
            guarded(self.can_receive, self.copy.wait_recv)

        def sent(self):
            guarded(self.can_send, self.copy.wait_send)

    pending = []

    def send(*args):
        message = Message(*args)
        pending.append(message)
        return message

    def neighbour(src, dst, di, dt, do=0):
        return send(
            src, dst, (o if do == 0 else other, i + di, t + dt),
            both(inside(i, di, n_in), inside(t, dt, n_tm)),
            both(inside(i, -di, n_in), inside(t, -dt, n_tm)),
        )

    lo_halo, hi_halo = pl.ds(0, APER), pl.ds(APER + rows, APER)
    body = pl.ds(APER, rows)
    first_rows, last_rows = pl.ds(APER, APER), pl.ds(rows, APER)

    cl[0] = jnp.full(cl.shape[1:], cls_ref[0], jnp.int32)
    class_msg = send(cl.at[0], cl.at[1], (other, i, t))
    entry = []
    for slot, xs in ((1, other_x), (0, own_x)):
        entry.append(neighbour(tr_ref.at[0, pl.ds(0, APER), xs], vt.at[slot, hi_halo], -1, 0, slot))
        entry.append(neighbour(tr_ref.at[0, pl.ds(rows - APER, APER), xs], vt.at[slot, lo_halo], 1, 0, slot))
    entry.append(send(tr_ref.at[0, :, other_x], vt.at[1, body], (other, i, t)))
    own_copy = pltpu.make_async_copy(tr_ref.at[0, :, own_x], vt.at[0, body], local_sem)
    own_copy.start()

    @pl.when(i == 0)
    def _():
        vt[:, 0:APER] = jnp.zeros_like(vt[:, 0:APER])
        p0[:, 0:APER] = jnp.zeros_like(p0[:, 0:APER])
        for u in range(2):
            ext[u, 0:APER] = jnp.zeros_like(ext[u, 0:APER])
            prev_strip[u, 0:APER] = jnp.zeros_like(prev_strip[u, 0:APER])
            next_strip[u, 0:APER] = jnp.zeros_like(next_strip[u, 0:APER])

    @pl.when(i == n_in - 1)
    def _():
        top = slice(APER + rows, 2 * APER + rows)
        vt[:, top] = jnp.zeros_like(vt[:, top])
        p0[:, top] = jnp.zeros_like(p0[:, top])
        for u in range(2):
            ext[u, top] = jnp.zeros_like(ext[u, top])
            prev_strip[u, top] = jnp.zeros_like(prev_strip[u, top])
            next_strip[u, top] = jnp.zeros_like(next_strip[u, top])

    @pl.when(jnp.logical_and(t == 0, i >= 0))
    def _():
        prev_strip[:, APER:APER + rows] = jnp.zeros_like(prev_strip[:, APER:APER + rows])

        @pl.when(i > 0)
        def _():
            prev_strip[:, 0:APER] = jnp.zeros_like(prev_strip[:, 0:APER])

        @pl.when(i < n_in - 1)
        def _():
            top = slice(APER + rows, 2 * APER + rows)
            prev_strip[:, top] = jnp.zeros_like(prev_strip[:, top])

    @pl.when(t == n_tm - 1)
    def _():
        next_strip[:, APER:APER + rows] = jnp.zeros_like(next_strip[:, APER:APER + rows])

        @pl.when(i > 0)
        def _():
            next_strip[:, 0:APER] = jnp.zeros_like(next_strip[:, 0:APER])

        @pl.when(i < n_in - 1)
        def _():
            top = slice(APER + rows, 2 * APER + rows)
            next_strip[:, top] = jnp.zeros_like(next_strip[:, top])

    sub = lax.broadcasted_iota(jnp.int32, (K, TB), 0)
    lane = lax.broadcasted_iota(jnp.int32, (K, TB), 1)
    groups = lax.broadcasted_iota(jnp.int32, (2 * TB // K, K, TB), 0)

    def build(slot):
        masks = [cl[slot] == c for c in range(st_ref.shape[0])]

        def one(j, carry):
            cols = pl.ds(pl.multiple_of(j * TB, TB), TB)
            for a in range(NAPER):
                start = jnp.zeros((K, TB), jnp.int32)
                taps = jnp.zeros((K, TB), jnp.float32)
                for c, mask in enumerate(masks):
                    row = jnp.broadcast_to(st_ref[c, a:a + 1, cols], (K, TB))
                    start = jnp.where(mask, row, start)
                    taps = jnp.where(mask, w_ref[c, a, :, cols], taps)
                reach = lane + LAG - start - sub
                group = lax.shift_right_logical(reach, 3)
                tap = jnp.bitwise_and(reach, K - 1)
                turned = jnp.zeros((K, TB), jnp.float32)
                for k in range(K):
                    turned = jnp.where(tap == k, jnp.broadcast_to(taps[k:k + 1], (K, TB)), turned)
                high = turned.astype(jnp.bfloat16).astype(jnp.float32)
                low = turned - high
                hit = groups == group[None]
                place = slice(slot * TB, (slot + 1) * TB)
                bh[a, j, :, place] = jnp.where(hit, high[None], 0.0).reshape(2 * TB, TB).astype(jnp.bfloat16)
                bl[a, j, :, place] = jnp.where(hit, low[None], 0.0).reshape(2 * TB, TB).astype(jnp.bfloat16)
            return carry

        lax.fori_loop(0, tiles, one, 0)

    build(0)
    class_msg.received()
    build(1)
    own_copy.wait()
    for message in entry:
        message.received()

    def apply(data, firsts, j, dims):
        high = data.astype(jnp.bfloat16).astype(jnp.float32)
        low = data - high
        total = None
        for a in range(NAPER):
            r0 = firsts[a]
            slab_high = high[r0:r0 + rows].reshape(flat, 2 * TB)
            slab_low = low[r0:r0 + rows].reshape(flat, 2 * TB)
            stacked = jnp.concatenate([slab_high, slab_low], axis=0).astype(jnp.bfloat16)
            main = lax.dot_general(stacked, bh[a, j], dims, preferred_element_type=jnp.float32)
            rest = lax.dot_general(
                slab_high.astype(jnp.bfloat16), bl[a, j], dims, preferred_element_type=jnp.float32
            )
            term = main[:flat] + (main[flat:] + rest)
            total = term if total is None else total + term
        return total

    def migrate(values, u):
        carried = None
        for j in range(tiles):
            cols = slice(j * TB, (j + 1) * TB)
            data = jnp.concatenate([values[0, :, :, cols], values[1, :, :, cols]], axis=2)
            part = apply(data, [2 * APER - a for a in range(NAPER)], j, (((1,), (1,)), ((), ())))
            head = part[:, :TB] if carried is None else part[:, :TB] + carried
            ext[u, APER:APER + rows, :, cols] = head.reshape(rows, xl, TB)
            carried = part[:, TB:]
        ext[u, APER:APER + rows, :, window:window + TB] = carried.reshape(rows, xl, TB)

    def demigrate(u, store):
        for j in range(tiles):
            data = img[u, :, :, j * TB:(j + 2) * TB]
            part = apply(data, list(range(NAPER)), j, (((1,), (0,)), ((), ())))
            store(j, part.reshape(rows, xl, 2 * TB))

    def swap_edges(u):
        messages = []
        for source, target, di in ((first_rows, hi_halo, -1), (last_rows, lo_halo, 1)):
            messages.append(neighbour(ext.at[u, source], ext.at[u, target], di, 0))
            messages.append(neighbour(
                ext.at[u, source, :, pl.ds(0, TB)], next_strip.at[u, target], di, -1))
            messages.append(neighbour(
                ext.at[u, source, :, pl.ds(window, TB)], prev_strip.at[u, target], di, 1))
        messages.append(neighbour(
            ext.at[u, body, :, pl.ds(0, TB)], next_strip.at[u, body], 0, -1))
        messages.append(neighbour(
            ext.at[u, body, :, pl.ds(window, TB)], prev_strip.at[u, body], 0, 1))
        for message in messages:
            message.received()

    def whole(u):
        earlier = ext[u, :, :, :TB] + prev_strip[u]
        earlier = jnp.where(t == 0, jnp.zeros_like(earlier), earlier)
        return [
            (slice(0, TB), earlier),
            (slice(TB, window), ext[u, :, :, TB:window]),
            (slice(window, window + TB), ext[u, :, :, window:] + next_strip[u]),
        ]

    def tile_sum(value):
        value = value.reshape(-1, xl, window)
        folded = sum(value[:, :, c * TB:(c + 1) * TB] for c in range(tiles))
        return jnp.sum(folded, axis=0)

    def start_total(turn, parts):
        for n, part in enumerate(parts):
            sa[turn, m, n] = part
        messages = []
        for d in range(1, plane):
            peer = lax.rem(m + d, plane)
            messages.append(send(
                sa.at[turn, m], sa.at[turn, m], (lax.div(peer, n_tm), i, lax.rem(peer, n_tm))))
        return messages

    def next_total(turn, messages):
        for message in messages:
            message.received()
        sb[turn, i] = sum(sa[turn, s] for s in range(plane))
        return [
            send(sb.at[turn, i], sb.at[turn, i], (o, lax.rem(i + d, n_in), t))
            for d in range(1, n_in)
        ]

    def end_total(turn, messages):
        for message in messages:
            message.received()
        total = sum(sb[turn, s] for s in range(n_in))
        return [
            jnp.sum(jnp.sum(total[n], axis=1, keepdims=True), axis=0, keepdims=True)
            for n in range(total.shape[0])
        ]

    def own_image(u):
        return img[u, APER:APER + rows, :, LAG:]

    migrate(vt, 0)
    swap_edges(0)
    for cols, value in whole(0):
        img[0, :, :, cols] = value
    mg0_msg = send(img.at[0, body, :, pl.ds(LAG, window)], mg.at[0], (other, i, t))

    def store_p0(j, part):
        for slot in range(2):
            p0[slot, APER:APER + rows, :, j * TB:(j + 1) * TB] = part[:, :, slot * TB:(slot + 1) * TB]

    demigrate(0, store_p0)
    halo = [
        neighbour(p0.at[:, first_rows], p0.at[:, hi_halo], -1, 0),
        neighbour(p0.at[:, last_rows], p0.at[:, lo_halo], 1, 0),
    ]
    own_p0 = p0[:, APER:APER + rows]
    zero_tile = jnp.zeros((xl, TB), jnp.float32)
    messages = start_total(0, [tile_sum(own_image(0) * own_image(0)), tile_sum(own_p0 * own_p0), zero_tile])
    px0_msg = send(p0.at[1, body], px.at[0], (other, i, t))
    for message in halo:
        message.received()
    messages = next_total(0, messages)
    migrate(p0, 1)
    swap_edges(1)
    gnorm, curvature, _ = end_total(0, messages)
    step0 = gnorm / curvature
    for cols, value in whole(1):
        img[1, :, :, cols] = img[0, :, :, cols] - step0[None] * value
    mg1_msg = send(img.at[1, body, :, pl.ds(LAG, window)], mg.at[1], (other, i, t))

    def store_p1(j, part):
        for slot in range(2):
            p1[slot, :, :, j * TB:(j + 1) * TB] = part[:, :, slot * TB:(slot + 1) * TB]

    demigrate(1, store_p1)
    px1_msg = send(p1.at[1], px.at[1], (other, i, t))
    own_p0 = p0[:, APER:APER + rows]
    own_p1 = p1[...]
    messages = start_total(1, [
        tile_sum(own_image(1) * own_image(1)), tile_sum(own_p1 * own_p1), tile_sum(own_p1 * own_p0)])
    messages = next_total(1, messages)
    gnew, square, cross = end_total(1, messages)
    beta = gnew / gnorm
    step1 = gnew / (square + 2.0 * beta * cross + beta * beta * curvature)
    step0, step1, beta = step0[None], step1[None], beta[None]

    def image_of(g0, g1):
        return step0 * g0 + step1 * (g1 + beta * g0)

    def residual_of(r0, a0, a1):
        return r0 - step0 * a0 - step1 * (a1 + beta * a0)

    mig_ref[:, own_x, :] = image_of(own_image(0), own_image(1))
    res_ref[0, :, own_x, :] = residual_of(tr_ref[0, :, own_x, :], p0[0, APER:APER + rows], p1[0])
    for message in (mg0_msg, px0_msg, mg1_msg, px1_msg):
        message.received()
    mig_ref[:, other_x, :] = image_of(mg[0], mg[1])
    res_ref[0, :, other_x, :] = residual_of(tr_ref[0, :, other_x, :], px[0], px[1])
    for message in pending:
        message.sent()


def on_device_pair(n_in, n_tm, traces, class_of_block, band_start, band_weights):
    rows, crosslines, window = traces.shape[1:]
    xl = crosslines // 2
    wide = rows + 2 * APER
    tiles = window // TB
    messages = 64
    f32 = jnp.float32
    vmem = pl.BlockSpec(memory_space=pltpu.VMEM)
    return pl.pallas_call(
        functools.partial(kernel, n_in, n_tm),
        out_shape=(
            jax.ShapeDtypeStruct((rows, crosslines, window), f32),
            jax.ShapeDtypeStruct((1, rows, crosslines, window), f32),
        ),
        in_specs=[pl.BlockSpec(memory_space=pltpu.SMEM), vmem, vmem, vmem],
        out_specs=(vmem, vmem),
        scratch_shapes=[
            pltpu.VMEM((2, wide, xl, window), f32),
            pltpu.VMEM((2, wide, xl, window), f32),
            pltpu.VMEM((2, rows, xl, window), f32),
            pltpu.VMEM((2, wide, xl, window + LAG), f32),
            pltpu.VMEM((2, wide, xl, TB), f32),
            pltpu.VMEM((2, wide, xl, TB), f32),
            pltpu.VMEM((2, wide, xl, window + LAG), f32),
            pltpu.VMEM((NAPER, tiles, 2 * TB, 2 * TB), jnp.bfloat16),
            pltpu.VMEM((NAPER, tiles, 2 * TB, 2 * TB), jnp.bfloat16),
            pltpu.VMEM((2, K, TB), jnp.int32),
            pltpu.VMEM((2, 2 * n_tm, 3, xl, TB), f32),
            pltpu.VMEM((2, n_in, 3, xl, TB), f32),
            pltpu.VMEM((2, rows, xl, window), f32),
            pltpu.VMEM((2, rows, xl, window), f32),
            pltpu.SemaphoreType.DMA,
            pltpu.SemaphoreType.DMA((messages,)),
            pltpu.SemaphoreType.DMA((messages,)),
        ],
        compiler_params=pltpu.CompilerParams(
            collective_id=0, has_side_effects=True, vmem_limit_bytes=40 * 1024 * 1024
        ),
    )(class_of_block, traces, band_start, band_weights)


def solution(mesh):
    placed = (
        P("offset", "inline", None, "tm"),
        P("offset"),
        P(None, None, "tm"),
        P(None, None, None, "tm"),
    )
    if mesh.shape["offset"] == 2:
        body = functools.partial(on_device_pair, mesh.shape["inline"], mesh.shape["tm"])
    else:
        body = on_device_general
    return jax.shard_map(
        body,
        mesh=mesh,
        in_specs=placed,
        out_specs=(P("inline", None, "tm"), P("offset", "inline", None, "tm")),
        check_vma=False,
    )
```

```python
import functools

import jax
import jax.numpy as jnp
from jax import lax
from jax.experimental import pallas as pl
from jax.experimental.pallas import tpu as pltpu
from jax.sharding import PartitionSpec as P

K = 8
LAG = 128
APER = 2
ITERS = 2


def with_halo(block, sides, width):
    for axis, dim in sides:
        count = lax.axis_size(axis)
        forward = [(i, i + 1) for i in range(count - 1)]
        backward = [(target, source) for source, target in forward]
        low = lax.ppermute(
            lax.slice_in_dim(block, block.shape[dim] - width, None, axis=dim), axis, forward
        )
        high = lax.ppermute(lax.slice_in_dim(block, 0, width, axis=dim), axis, backward)
        block = jnp.concatenate([low, block, high], axis=dim)
    return block


def shifted(shard, axis, by):
    count = lax.axis_size(axis)
    pairs = [(i, i + by) for i in range(count) if 0 <= i + by < count]
    return lax.ppermute(shard, axis, pairs)


def widen_inline(field):
    return with_halo(field, (("inline", 1),), APER)


def totalled(value):
    return lax.psum(value, ("offset", "inline", "tm"))


def on_device_general(traces, class_of_block, band_start, band_weights):
    own_class = class_of_block[0]
    weights = lax.dynamic_index_in_dim(band_weights, own_class, 0, keepdims=False)
    starts = lax.dynamic_index_in_dim(band_start, own_class, 0, keepdims=False)
    inlines = traces.shape[1]
    crosslines = traces.shape[2]
    window = traces.shape[3]
    flat_rows = inlines * crosslines
    sample_rows = jnp.arange(window, dtype=jnp.int32)[:, None]
    sample_cols = jnp.arange(window + LAG, dtype=jnp.int32)[None, :]
    band_list = []
    for aper_index in range(2 * APER + 1):
        band_matrix = jnp.zeros((window, window + LAG), jnp.float32)
        for tap_index in range(K):
            target = sample_rows - starts[aper_index][:, None] - tap_index + LAG
            band_matrix = band_matrix + jnp.where(
                sample_cols == target, weights[aper_index, tap_index][:, None], 0.0
            )
        band_list.append(band_matrix)

    def migrate_block(values):
        widened = widen_inline(values)[0]
        result_sum = jnp.zeros((flat_rows, window + LAG), jnp.float32)
        for aper_index in range(2 * APER + 1):
            first = 2 * APER - aper_index
            slab_rows = widened[first : first + inlines].reshape(flat_rows, window)
            result_sum = result_sum + jnp.dot(
                slab_rows,
                band_list[aper_index],
                precision=lax.Precision.HIGHEST,
                preferred_element_type=jnp.float32,
            )
        result_sum = result_sum.reshape(inlines, crosslines, window + LAG)
        later_part = shifted(result_sum[:, :, :LAG], "tm", -1)
        own_part = result_sum[:, :, LAG:]
        return own_part.at[:, :, window - LAG :].add(later_part)

    def migrate(values):
        partial_image = migrate_block(values)
        gradient = lax.psum(partial_image, "offset")
        grad_norm = totalled(jnp.sum(gradient * gradient)) / lax.axis_size("offset")
        return (gradient, grad_norm)

    migrated = jnp.zeros((inlines, crosslines, window), jnp.float32)
    residual = traces
    gradient, grad_norm = migrate(residual)
    direction = gradient
    for iteration in range(ITERS):
        demigrate_widened = widen_inline(direction[None])[0]
        earlier = shifted(demigrate_widened[:, :, window - LAG :], "tm", 1)
        full_block = jnp.concatenate([earlier, demigrate_widened], axis=2)
        demigrate_result_sum = jnp.zeros((flat_rows, window), jnp.float32)
        for demigrate_aper_index in range(2 * APER + 1):
            demigrate_slab_rows = full_block[
                demigrate_aper_index : demigrate_aper_index + inlines
            ].reshape(flat_rows, window + LAG)
            demigrate_result_sum = demigrate_result_sum + lax.dot_general(
                demigrate_slab_rows,
                band_list[demigrate_aper_index],
                (((1,), (1,)), ((), ())),
                precision=lax.Precision.HIGHEST,
                preferred_element_type=jnp.float32,
            )
        projected = demigrate_result_sum.reshape(1, inlines, crosslines, window)
        curvature = totalled(jnp.sum(projected * projected))
        step_size = grad_norm / curvature
        migrated = migrated + step_size * direction
        residual = residual - step_size * projected
        if iteration + 1 < ITERS:
            gradient, grad_new = migrate(residual)
            direction = gradient + grad_new / grad_norm * direction
            grad_norm = grad_new
    return (migrated, residual)


TB = 128
MESH = pl.DeviceIdType.MESH
NAPER = 2 * APER + 1


def kernel(
    n_in, n_tm,
    cls_ref, tr_ref, st_hbm, w_hbm, mig_ref, res_ref,
    vt, p0, p1, ext, prev_strip, next_strip, img, bh, bl, cl, sa, sb, mg, px,
    st_ref, w_ref, spare, local_sem, send_sem, recv_sem,
):
    o = lax.axis_index("offset")
    i = lax.axis_index("inline")
    t = lax.axis_index("tm")
    other = 1 - o
    rows, window = tr_ref.shape[1], tr_ref.shape[3]
    xl = tr_ref.shape[2] // 2
    tiles = window // TB
    flat = rows * xl
    own_x = pl.ds(pl.multiple_of(o * xl, xl), xl)
    other_x = pl.ds(pl.multiple_of(other * xl, xl), xl)
    plane = 2 * n_tm
    m = o * n_tm + t

    start_copy = pltpu.make_async_copy(st_hbm, st_ref, local_sem.at[0])
    weight_copy = pltpu.make_async_copy(w_hbm, w_ref, local_sem.at[1])
    own_copy = pltpu.make_async_copy(tr_ref.at[0, :, own_x], vt.at[0, pl.ds(APER, rows)], local_sem.at[2])
    spare_copy = pltpu.make_async_copy(tr_ref.at[0, :, other_x], spare, local_sem.at[3])
    local_copies = (start_copy, weight_copy, own_copy, spare_copy)

    barrier = pltpu.get_barrier_semaphore()
    greeted = []
    for d in range(1, plane):
        peer = lax.rem(m + d, plane)
        greeted.append((lax.div(peer, n_tm), i, lax.rem(peer, n_tm)))
    for d in range(1, n_in):
        greeted.append((o, lax.rem(i + d, n_in), t))
    for di in sorted({1 % n_in, n_in - 1} - {0}):
        greeted.append((other, lax.rem(i + di, n_in), t))
        for dt in sorted({1 % n_tm, n_tm - 1} - {0}):
            greeted.append((o, lax.rem(i + di, n_in), lax.rem(t + dt, n_tm)))
    for device in greeted:
        pl.semaphore_signal(barrier, inc=1, device_id=device, device_id_type=MESH)
    for copy in local_copies:
        copy.start()
    pl.semaphore_wait(barrier, len(greeted))

    used = [0]

    def both(first, second):
        if first is None:
            return second
        if second is None:
            return first
        return jnp.logical_and(first, second)

    def inside(index, step, count):
        if step == 0:
            return None
        if step > 0:
            return index + step < count
        return index + step >= 0

    def guarded(condition, action):
        if condition is None:
            action()
        else:
            pl.when(condition)(action)

    class Message:
        def __init__(self, src, dst, device, can_send=None, can_receive=None):
            number = used[0]
            used[0] += 1
            self.copy = pltpu.make_async_remote_copy(
                src_ref=src, dst_ref=dst,
                send_sem=send_sem.at[number], recv_sem=recv_sem.at[number],
                device_id=device, device_id_type=MESH,
            )
            self.can_send, self.can_receive = can_send, can_receive
            guarded(can_send, self.copy.start)

        def received(self):
            guarded(self.can_receive, self.copy.wait_recv)

        def sent(self):
            guarded(self.can_send, self.copy.wait_send)

    pending = []

    def send(*args):
        message = Message(*args)
        pending.append(message)
        return message

    def neighbour(src, dst, di, dt, do=0):
        return send(
            src, dst, (o if do == 0 else other, i + di, t + dt),
            both(inside(i, di, n_in), inside(t, dt, n_tm)),
            both(inside(i, -di, n_in), inside(t, -dt, n_tm)),
        )

    lo_halo, hi_halo = pl.ds(0, APER), pl.ds(APER + rows, APER)
    body = pl.ds(APER, rows)
    first_rows, last_rows = pl.ds(APER, APER), pl.ds(rows, APER)

    cl[0] = jnp.full(cl.shape[1:], cls_ref[0], jnp.int32)
    class_msg = send(cl.at[0], cl.at[1], (other, i, t))
    entry = []
    for slot, xs in ((1, other_x), (0, own_x)):
        entry.append(neighbour(tr_ref.at[0, pl.ds(0, APER), xs], vt.at[slot, hi_halo], -1, 0, slot))
        entry.append(neighbour(tr_ref.at[0, pl.ds(rows - APER, APER), xs], vt.at[slot, lo_halo], 1, 0, slot))
    entry.append(send(tr_ref.at[0, :, other_x], vt.at[1, body], (other, i, t)))

    @pl.when(i == 0)
    def _():
        vt[:, 0:APER] = jnp.zeros_like(vt[:, 0:APER])
        p0[:, 0:APER] = jnp.zeros_like(p0[:, 0:APER])
        for u in range(2):
            ext[u, 0:APER] = jnp.zeros_like(ext[u, 0:APER])
            prev_strip[u, 0:APER] = jnp.zeros_like(prev_strip[u, 0:APER])
            next_strip[u, 0:APER] = jnp.zeros_like(next_strip[u, 0:APER])

    @pl.when(i == n_in - 1)
    def _():
        top = slice(APER + rows, 2 * APER + rows)
        vt[:, top] = jnp.zeros_like(vt[:, top])
        p0[:, top] = jnp.zeros_like(p0[:, top])
        for u in range(2):
            ext[u, top] = jnp.zeros_like(ext[u, top])
            prev_strip[u, top] = jnp.zeros_like(prev_strip[u, top])
            next_strip[u, top] = jnp.zeros_like(next_strip[u, top])

    @pl.when(jnp.logical_and(t == 0, i >= 0))
    def _():
        prev_strip[:, APER:APER + rows] = jnp.zeros_like(prev_strip[:, APER:APER + rows])

        @pl.when(i > 0)
        def _():
            prev_strip[:, 0:APER] = jnp.zeros_like(prev_strip[:, 0:APER])

        @pl.when(i < n_in - 1)
        def _():
            top = slice(APER + rows, 2 * APER + rows)
            prev_strip[:, top] = jnp.zeros_like(prev_strip[:, top])

    @pl.when(t == n_tm - 1)
    def _():
        next_strip[:, APER:APER + rows] = jnp.zeros_like(next_strip[:, APER:APER + rows])

        @pl.when(i > 0)
        def _():
            next_strip[:, 0:APER] = jnp.zeros_like(next_strip[:, 0:APER])

        @pl.when(i < n_in - 1)
        def _():
            top = slice(APER + rows, 2 * APER + rows)
            next_strip[:, top] = jnp.zeros_like(next_strip[:, top])

    sub = lax.broadcasted_iota(jnp.int32, (K, TB), 0)
    lane = lax.broadcasted_iota(jnp.int32, (K, TB), 1)
    groups = lax.broadcasted_iota(jnp.int32, (2 * TB // K, K, TB), 0)

    def build(slot):
        masks = [cl[slot] == c for c in range(st_ref.shape[1])]

        def one(j, carry):
            cols = pl.ds(pl.multiple_of(j * TB, TB), TB)
            for a in range(NAPER):
                start = jnp.zeros((K, TB), jnp.int32)
                taps = jnp.zeros((K, TB), jnp.float32)
                for c, mask in enumerate(masks):
                    row = jnp.broadcast_to(st_ref[a, c:c + 1, cols], (K, TB))
                    start = jnp.where(mask, row, start)
                    taps = jnp.where(mask, w_ref[c, a, :, cols], taps)
                reach = lane + LAG - start - sub
                group = lax.shift_right_logical(reach, 3)
                tap = jnp.bitwise_and(reach, K - 1)
                turned = jnp.zeros((K, TB), jnp.float32)
                for k in range(K):
                    turned = jnp.where(tap == k, jnp.broadcast_to(taps[k:k + 1], (K, TB)), turned)
                high = turned.astype(jnp.bfloat16).astype(jnp.float32)
                low = turned - high
                hit = groups == group[None]
                place = slice(slot * TB, (slot + 1) * TB)
                bh[a, j, :, place] = jnp.where(hit, high[None], 0.0).reshape(2 * TB, TB).astype(jnp.bfloat16)
                bl[a, j, :, place] = jnp.where(hit, low[None], 0.0).reshape(2 * TB, TB).astype(jnp.bfloat16)
            return carry

        lax.fori_loop(0, tiles, one, 0)

    start_copy.wait()
    weight_copy.wait()
    build(0)
    class_msg.received()
    build(1)
    own_copy.wait()
    for message in entry:
        message.received()

    def apply(data, firsts, j, dims):
        high = data.astype(jnp.bfloat16).astype(jnp.float32)
        low = data - high
        total = None
        for a in range(NAPER):
            r0 = firsts[a]
            slab_high = high[r0:r0 + rows].reshape(flat, 2 * TB)
            slab_low = low[r0:r0 + rows].reshape(flat, 2 * TB)
            stacked = jnp.concatenate([slab_high, slab_low], axis=0).astype(jnp.bfloat16)
            main = lax.dot_general(stacked, bh[a, j], dims, preferred_element_type=jnp.float32)
            rest = lax.dot_general(
                slab_high.astype(jnp.bfloat16), bl[a, j], dims, preferred_element_type=jnp.float32
            )
            term = main[:flat] + (main[flat:] + rest)
            total = term if total is None else total + term
        return total

    def migrate(values, u):
        carried = None
        for j in range(tiles):
            cols = slice(j * TB, (j + 1) * TB)
            data = jnp.concatenate([values[0, :, :, cols], values[1, :, :, cols]], axis=2)
            part = apply(data, [2 * APER - a for a in range(NAPER)], j, (((1,), (1,)), ((), ())))
            head = part[:, :TB] if carried is None else part[:, :TB] + carried
            ext[u, APER:APER + rows, :, cols] = head.reshape(rows, xl, TB)
            carried = part[:, TB:]
        ext[u, APER:APER + rows, :, window:window + TB] = carried.reshape(rows, xl, TB)

    def demigrate(u, store):
        for j in range(tiles):
            data = img[u, :, :, j * TB:(j + 2) * TB]
            part = apply(data, list(range(NAPER)), j, (((1,), (0,)), ((), ())))
            store(j, part.reshape(rows, xl, 2 * TB))

    def swap_edges(u):
        messages = []
        for source, target, di in ((first_rows, hi_halo, -1), (last_rows, lo_halo, 1)):
            messages.append(neighbour(ext.at[u, source], ext.at[u, target], di, 0))
            messages.append(neighbour(
                ext.at[u, source, :, pl.ds(0, TB)], next_strip.at[u, target], di, -1))
            messages.append(neighbour(
                ext.at[u, source, :, pl.ds(window, TB)], prev_strip.at[u, target], di, 1))
        messages.append(neighbour(
            ext.at[u, body, :, pl.ds(0, TB)], next_strip.at[u, body], 0, -1))
        messages.append(neighbour(
            ext.at[u, body, :, pl.ds(window, TB)], prev_strip.at[u, body], 0, 1))
        for message in messages:
            message.received()

    def whole(u):
        earlier = ext[u, :, :, :TB] + prev_strip[u]
        earlier = jnp.where(t == 0, jnp.zeros_like(earlier), earlier)
        return [
            (slice(0, TB), earlier),
            (slice(TB, window), ext[u, :, :, TB:window]),
            (slice(window, window + TB), ext[u, :, :, window:] + next_strip[u]),
        ]

    def tile_sum(value):
        value = value.reshape(-1, xl, window)
        folded = sum(value[:, :, c * TB:(c + 1) * TB] for c in range(tiles))
        return jnp.sum(folded, axis=0)

    def start_total(turn, parts):
        for n, part in enumerate(parts):
            sa[turn, m, n:n + 1] = jnp.sum(part, axis=0, keepdims=True)
        sa[turn, m, len(parts):] = jnp.zeros((K - len(parts), TB), jnp.float32)
        messages = []
        for d in range(1, plane):
            peer = lax.rem(m + d, plane)
            messages.append(send(
                sa.at[turn, m], sa.at[turn, m], (lax.div(peer, n_tm), i, lax.rem(peer, n_tm))))
        return messages

    def next_total(turn, messages):
        for message in messages:
            message.received()
        sb[turn, i] = sum(sa[turn, s] for s in range(plane))
        return [
            send(sb.at[turn, i], sb.at[turn, i], (o, lax.rem(i + d, n_in), t))
            for d in range(1, n_in)
        ]

    def end_total(turn, messages):
        for message in messages:
            message.received()
        total = sum(sb[turn, s] for s in range(n_in))
        total = jnp.sum(total, axis=1, keepdims=True)
        return [total[n:n + 1] for n in range(3)]

    def own_image(u):
        return img[u, APER:APER + rows, :, LAG:]

    migrate(vt, 0)
    swap_edges(0)
    for cols, value in whole(0):
        img[0, :, :, cols] = value
    mg0_msg = send(img.at[0, body, :, pl.ds(LAG, window)], mg.at[0], (other, i, t))

    def store_p0(j, part):
        for slot in range(2):
            p0[slot, APER:APER + rows, :, j * TB:(j + 1) * TB] = part[:, :, slot * TB:(slot + 1) * TB]

    demigrate(0, store_p0)
    halo = [
        neighbour(p0.at[:, first_rows], p0.at[:, hi_halo], -1, 0),
        neighbour(p0.at[:, last_rows], p0.at[:, lo_halo], 1, 0),
    ]
    own_p0 = p0[:, APER:APER + rows]
    messages = start_total(0, [tile_sum(own_image(0) * own_image(0)), tile_sum(own_p0 * own_p0)])
    px0_msg = send(p0.at[1, body], px.at[0], (other, i, t))
    for message in halo:
        message.received()
    messages = next_total(0, messages)
    migrate(p0, 1)
    swap_edges(1)
    gnorm, curvature, _ = end_total(0, messages)
    step0 = gnorm / curvature
    for cols, value in whole(1):
        img[1, :, :, cols] = img[0, :, :, cols] - step0[None] * value
    mg1_msg = send(img.at[1, body, :, pl.ds(LAG, window)], mg.at[1], (other, i, t))

    def store_p1(j, part):
        for slot in range(2):
            p1[slot, :, :, j * TB:(j + 1) * TB] = part[:, :, slot * TB:(slot + 1) * TB]
        if j < tiles - 1:
            send_p1(j)

    px1_msgs = []

    def send_p1(j):
        cols = pl.ds(j * TB, TB)
        px1_msgs.append(send(p1.at[1, :, :, cols], px.at[1, :, :, cols], (other, i, t)))

    demigrate(1, store_p1)
    own_p0 = p0[:, APER:APER + rows]
    own_p1 = p1[...]
    messages = start_total(1, [
        tile_sum(own_image(1) * own_image(1)), tile_sum(own_p1 * own_p1), tile_sum(own_p1 * own_p0)])
    send_p1(tiles - 1)
    messages = next_total(1, messages)
    gnew, square, cross = end_total(1, messages)
    beta = gnew / gnorm
    step1 = gnew / (square + 2.0 * beta * cross + beta * beta * curvature)
    step0, step1, beta = step0[None], step1[None], beta[None]

    def image_of(g0, g1):
        return step0 * g0 + step1 * (g1 + beta * g0)

    def residual_of(r0, a0, a1):
        return r0 - step0 * a0 - step1 * (a1 + beta * a0)

    mig_ref[:, own_x, :] = image_of(own_image(0), own_image(1))
    res_ref[0, :, own_x, :] = residual_of(vt[0, APER:APER + rows], p0[0, APER:APER + rows], p1[0])
    spare_copy.wait()
    for message in (mg0_msg, px0_msg, mg1_msg, *px1_msgs):
        message.received()
    mig_ref[:, other_x, :] = image_of(mg[0], mg[1])
    res_ref[0, :, other_x, :] = residual_of(spare[...], px[0], px[1])
    for message in pending:
        message.sent()


def on_device_pair(n_in, n_tm, traces, class_of_block, band_start, band_weights):
    rows, crosslines, window = traces.shape[1:]
    xl = crosslines // 2
    wide = rows + 2 * APER
    tiles = window // TB
    messages = 64
    f32 = jnp.float32
    vmem = pl.BlockSpec(memory_space=pltpu.VMEM)
    hbm = pl.BlockSpec(memory_space=pltpu.HBM)
    return pl.pallas_call(
        functools.partial(kernel, n_in, n_tm),
        out_shape=(
            jax.ShapeDtypeStruct((rows, crosslines, window), f32),
            jax.ShapeDtypeStruct((1, rows, crosslines, window), f32),
        ),
        in_specs=[pl.BlockSpec(memory_space=pltpu.SMEM), hbm, hbm, hbm],
        out_specs=(vmem, vmem),
        scratch_shapes=[
            pltpu.VMEM((2, wide, xl, window), f32),
            pltpu.VMEM((2, wide, xl, window), f32),
            pltpu.VMEM((2, rows, xl, window), f32),
            pltpu.VMEM((2, wide, xl, window + LAG), f32),
            pltpu.VMEM((2, wide, xl, TB), f32),
            pltpu.VMEM((2, wide, xl, TB), f32),
            pltpu.VMEM((2, wide, xl, window + LAG), f32),
            pltpu.VMEM((NAPER, tiles, 2 * TB, 2 * TB), jnp.bfloat16),
            pltpu.VMEM((NAPER, tiles, 2 * TB, 2 * TB), jnp.bfloat16),
            pltpu.VMEM((2, K, TB), jnp.int32),
            pltpu.VMEM((2, 2 * n_tm, K, TB), f32),
            pltpu.VMEM((2, n_in, K, TB), f32),
            pltpu.VMEM((2, rows, xl, window), f32),
            pltpu.VMEM((2, rows, xl, window), f32),
            pltpu.VMEM((NAPER,) + band_start.shape[:1] + (window,), jnp.int32),
            pltpu.VMEM(band_weights.shape, f32),
            pltpu.VMEM((rows, xl, window), f32),
            pltpu.SemaphoreType.DMA((4,)),
            pltpu.SemaphoreType.DMA((messages,)),
            pltpu.SemaphoreType.DMA((messages,)),
        ],
        compiler_params=pltpu.CompilerParams(
            collective_id=0, has_side_effects=True, vmem_limit_bytes=60 * 1024 * 1024
        ),
    )(class_of_block, traces, band_start.transpose(1, 0, 2), band_weights)


def solution(mesh):
    placed = (
        P("offset", "inline", None, "tm"),
        P("offset"),
        P(None, None, "tm"),
        P(None, None, None, "tm"),
    )
    if mesh.shape["offset"] == 2:
        body = functools.partial(on_device_pair, mesh.shape["inline"], mesh.shape["tm"])
    else:
        body = on_device_general
    return jax.shard_map(
        body,
        mesh=mesh,
        in_specs=placed,
        out_specs=(P("inline", None, "tm"), P("offset", "inline", None, "tm")),
        check_vma=False,
    )
```

```python
import functools

import jax
import jax.numpy as jnp
from jax import lax
from jax.experimental import pallas as pl
from jax.experimental.pallas import tpu as pltpu
from jax.sharding import PartitionSpec as P

K = 8
LAG = 128
APER = 2
ITERS = 2


def with_halo(block, sides, width):
    for axis, dim in sides:
        count = lax.axis_size(axis)
        forward = [(i, i + 1) for i in range(count - 1)]
        backward = [(target, source) for source, target in forward]
        low = lax.ppermute(
            lax.slice_in_dim(block, block.shape[dim] - width, None, axis=dim), axis, forward
        )
        high = lax.ppermute(lax.slice_in_dim(block, 0, width, axis=dim), axis, backward)
        block = jnp.concatenate([low, block, high], axis=dim)
    return block


def shifted(shard, axis, by):
    count = lax.axis_size(axis)
    pairs = [(i, i + by) for i in range(count) if 0 <= i + by < count]
    return lax.ppermute(shard, axis, pairs)


def widen_inline(field):
    return with_halo(field, (("inline", 1),), APER)


def totalled(value):
    return lax.psum(value, ("offset", "inline", "tm"))


def on_device_general(traces, class_of_block, band_start, band_weights):
    own_class = class_of_block[0]
    weights = lax.dynamic_index_in_dim(band_weights, own_class, 0, keepdims=False)
    starts = lax.dynamic_index_in_dim(band_start, own_class, 0, keepdims=False)
    inlines = traces.shape[1]
    crosslines = traces.shape[2]
    window = traces.shape[3]
    flat_rows = inlines * crosslines
    sample_rows = jnp.arange(window, dtype=jnp.int32)[:, None]
    sample_cols = jnp.arange(window + LAG, dtype=jnp.int32)[None, :]
    band_list = []
    for aper_index in range(2 * APER + 1):
        band_matrix = jnp.zeros((window, window + LAG), jnp.float32)
        for tap_index in range(K):
            target = sample_rows - starts[aper_index][:, None] - tap_index + LAG
            band_matrix = band_matrix + jnp.where(
                sample_cols == target, weights[aper_index, tap_index][:, None], 0.0
            )
        band_list.append(band_matrix)

    def migrate_block(values):
        widened = widen_inline(values)[0]
        result_sum = jnp.zeros((flat_rows, window + LAG), jnp.float32)
        for aper_index in range(2 * APER + 1):
            first = 2 * APER - aper_index
            slab_rows = widened[first : first + inlines].reshape(flat_rows, window)
            result_sum = result_sum + jnp.dot(
                slab_rows,
                band_list[aper_index],
                precision=lax.Precision.HIGHEST,
                preferred_element_type=jnp.float32,
            )
        result_sum = result_sum.reshape(inlines, crosslines, window + LAG)
        later_part = shifted(result_sum[:, :, :LAG], "tm", -1)
        own_part = result_sum[:, :, LAG:]
        return own_part.at[:, :, window - LAG :].add(later_part)

    def migrate(values):
        partial_image = migrate_block(values)
        gradient = lax.psum(partial_image, "offset")
        grad_norm = totalled(jnp.sum(gradient * gradient)) / lax.axis_size("offset")
        return (gradient, grad_norm)

    migrated = jnp.zeros((inlines, crosslines, window), jnp.float32)
    residual = traces
    gradient, grad_norm = migrate(residual)
    direction = gradient
    for iteration in range(ITERS):
        demigrate_widened = widen_inline(direction[None])[0]
        earlier = shifted(demigrate_widened[:, :, window - LAG :], "tm", 1)
        full_block = jnp.concatenate([earlier, demigrate_widened], axis=2)
        demigrate_result_sum = jnp.zeros((flat_rows, window), jnp.float32)
        for demigrate_aper_index in range(2 * APER + 1):
            demigrate_slab_rows = full_block[
                demigrate_aper_index : demigrate_aper_index + inlines
            ].reshape(flat_rows, window + LAG)
            demigrate_result_sum = demigrate_result_sum + lax.dot_general(
                demigrate_slab_rows,
                band_list[demigrate_aper_index],
                (((1,), (1,)), ((), ())),
                precision=lax.Precision.HIGHEST,
                preferred_element_type=jnp.float32,
            )
        projected = demigrate_result_sum.reshape(1, inlines, crosslines, window)
        curvature = totalled(jnp.sum(projected * projected))
        step_size = grad_norm / curvature
        migrated = migrated + step_size * direction
        residual = residual - step_size * projected
        if iteration + 1 < ITERS:
            gradient, grad_new = migrate(residual)
            direction = gradient + grad_new / grad_norm * direction
            grad_norm = grad_new
    return (migrated, residual)


TB = 128
MESH = pl.DeviceIdType.MESH
NAPER = 2 * APER + 1


def kernel(
    n_in, n_tm,
    cls_ref, tr_ref, st_hbm, w_hbm, mig_ref, res_ref,
    vt, p0, p1, ext, prev_strip, next_strip, img, bh, bl, cl, sa, sb, mg, px,
    st_ref, w_ref, spare, local_sem, send_sem, recv_sem,
):
    o = lax.axis_index("offset")
    i = lax.axis_index("inline")
    t = lax.axis_index("tm")
    other = 1 - o
    rows, window = tr_ref.shape[1], tr_ref.shape[3]
    xl = tr_ref.shape[2] // 2
    tiles = window // TB
    flat = rows * xl
    own_x = pl.ds(pl.multiple_of(o * xl, xl), xl)
    other_x = pl.ds(pl.multiple_of(other * xl, xl), xl)
    plane = 2 * n_tm
    m = o * n_tm + t

    start_copy = pltpu.make_async_copy(st_hbm, st_ref, local_sem.at[0])
    weight_copy = pltpu.make_async_copy(w_hbm, w_ref, local_sem.at[1])
    own_copy = pltpu.make_async_copy(tr_ref.at[0, :, own_x], vt.at[0, pl.ds(APER, rows)], local_sem.at[2])
    spare_copy = pltpu.make_async_copy(tr_ref.at[0, :, other_x], spare, local_sem.at[3])
    local_copies = (start_copy, weight_copy, own_copy, spare_copy)

    barrier = pltpu.get_barrier_semaphore()
    greeted = []
    for d in range(1, plane):
        peer = lax.rem(m + d, plane)
        greeted.append((lax.div(peer, n_tm), i, lax.rem(peer, n_tm)))
    for d in range(1, n_in):
        greeted.append((o, lax.rem(i + d, n_in), t))
    for di in sorted({1 % n_in, n_in - 1} - {0}):
        greeted.append((other, lax.rem(i + di, n_in), t))
        for dt in sorted({1 % n_tm, n_tm - 1} - {0}):
            greeted.append((o, lax.rem(i + di, n_in), lax.rem(t + dt, n_tm)))
    for device in greeted:
        pl.semaphore_signal(barrier, inc=1, device_id=device, device_id_type=MESH)
    for copy in local_copies:
        copy.start()
    pl.semaphore_wait(barrier, len(greeted))

    used = [0]

    def both(first, second):
        if first is None:
            return second
        if second is None:
            return first
        return jnp.logical_and(first, second)

    def inside(index, step, count):
        if step == 0:
            return None
        if step > 0:
            return index + step < count
        return index + step >= 0

    def guarded(condition, action):
        if condition is None:
            action()
        else:
            pl.when(condition)(action)

    class Message:
        def __init__(self, src, dst, device, can_send=None, can_receive=None):
            number = used[0]
            used[0] += 1
            self.copy = pltpu.make_async_remote_copy(
                src_ref=src, dst_ref=dst,
                send_sem=send_sem.at[number], recv_sem=recv_sem.at[number],
                device_id=device, device_id_type=MESH,
            )
            self.can_send, self.can_receive = can_send, can_receive
            guarded(can_send, self.copy.start)

        def received(self):
            guarded(self.can_receive, self.copy.wait_recv)

        def sent(self):
            guarded(self.can_send, self.copy.wait_send)

    pending = []

    def send(*args):
        message = Message(*args)
        pending.append(message)
        return message

    def neighbour(src, dst, di, dt, do=0):
        return send(
            src, dst, (o if do == 0 else other, i + di, t + dt),
            both(inside(i, di, n_in), inside(t, dt, n_tm)),
            both(inside(i, -di, n_in), inside(t, -dt, n_tm)),
        )

    lo_halo, hi_halo = pl.ds(0, APER), pl.ds(APER + rows, APER)
    body = pl.ds(APER, rows)
    first_rows, last_rows = pl.ds(APER, APER), pl.ds(rows, APER)

    cl[0] = jnp.full(cl.shape[1:], cls_ref[0], jnp.int32)
    class_msg = send(cl.at[0], cl.at[1], (other, i, t))
    entry = {}
    part = max(1, tiles // 2) * TB
    for begin in range(0, window, part):
        piece = pl.ds(begin, min(part, window - begin))
        arriving = entry[begin // TB] = []
        for slot, xs in ((1, other_x), (0, own_x)):
            arriving.append(neighbour(
                tr_ref.at[0, pl.ds(0, APER), xs, piece], vt.at[slot, hi_halo, :, piece], -1, 0, slot))
            arriving.append(neighbour(
                tr_ref.at[0, pl.ds(rows - APER, APER), xs, piece],
                vt.at[slot, lo_halo, :, piece], 1, 0, slot))
        arriving.append(send(
            tr_ref.at[0, :, other_x, piece], vt.at[1, body, :, piece], (other, i, t)))

    @pl.when(i == 0)
    def _():
        vt[:, 0:APER] = jnp.zeros_like(vt[:, 0:APER])
        p0[:, 0:APER] = jnp.zeros_like(p0[:, 0:APER])
        for u in range(2):
            ext[u, 0:APER] = jnp.zeros_like(ext[u, 0:APER])
            prev_strip[u, 0:APER] = jnp.zeros_like(prev_strip[u, 0:APER])
            next_strip[u, 0:APER] = jnp.zeros_like(next_strip[u, 0:APER])

    @pl.when(i == n_in - 1)
    def _():
        top = slice(APER + rows, 2 * APER + rows)
        vt[:, top] = jnp.zeros_like(vt[:, top])
        p0[:, top] = jnp.zeros_like(p0[:, top])
        for u in range(2):
            ext[u, top] = jnp.zeros_like(ext[u, top])
            prev_strip[u, top] = jnp.zeros_like(prev_strip[u, top])
            next_strip[u, top] = jnp.zeros_like(next_strip[u, top])

    @pl.when(jnp.logical_and(t == 0, i >= 0))
    def _():
        prev_strip[:, APER:APER + rows] = jnp.zeros_like(prev_strip[:, APER:APER + rows])

        @pl.when(i > 0)
        def _():
            prev_strip[:, 0:APER] = jnp.zeros_like(prev_strip[:, 0:APER])

        @pl.when(i < n_in - 1)
        def _():
            top = slice(APER + rows, 2 * APER + rows)
            prev_strip[:, top] = jnp.zeros_like(prev_strip[:, top])

    @pl.when(t == n_tm - 1)
    def _():
        next_strip[:, APER:APER + rows] = jnp.zeros_like(next_strip[:, APER:APER + rows])

        @pl.when(i > 0)
        def _():
            next_strip[:, 0:APER] = jnp.zeros_like(next_strip[:, 0:APER])

        @pl.when(i < n_in - 1)
        def _():
            top = slice(APER + rows, 2 * APER + rows)
            next_strip[:, top] = jnp.zeros_like(next_strip[:, top])

    sub = lax.broadcasted_iota(jnp.int32, (K, TB), 0)
    lane = lax.broadcasted_iota(jnp.int32, (K, TB), 1)
    groups = lax.broadcasted_iota(jnp.int32, (2 * TB // K, K, TB), 0)

    def build(slot):
        masks = [cl[slot] == c for c in range(st_ref.shape[1])]

        def one(j, carry):
            cols = pl.ds(pl.multiple_of(j * TB, TB), TB)
            for a in range(NAPER):
                start = jnp.zeros((K, TB), jnp.int32)
                taps = jnp.zeros((K, TB), jnp.float32)
                for c, mask in enumerate(masks):
                    row = jnp.broadcast_to(st_ref[a, c:c + 1, cols], (K, TB))
                    start = jnp.where(mask, row, start)
                    taps = jnp.where(mask, w_ref[c, a, :, cols], taps)
                reach = lane + LAG - start - sub
                group = lax.shift_right_logical(reach, 3)
                tap = jnp.bitwise_and(reach, K - 1)
                turned = jnp.zeros((K, TB), jnp.float32)
                for k in range(K):
                    turned = jnp.where(tap == k, jnp.broadcast_to(taps[k:k + 1], (K, TB)), turned)
                high = turned.astype(jnp.bfloat16).astype(jnp.float32)
                low = turned - high
                hit = groups == group[None]
                place = slice(slot * TB, (slot + 1) * TB)
                bh[a, j, :, place] = jnp.where(hit, high[None], 0.0).reshape(2 * TB, TB).astype(jnp.bfloat16)
                bl[a, j, :, place] = jnp.where(hit, low[None], 0.0).reshape(2 * TB, TB).astype(jnp.bfloat16)
            return carry

        lax.fori_loop(0, tiles, one, 0)

    start_copy.wait()
    weight_copy.wait()
    build(0)
    class_msg.received()
    build(1)
    own_copy.wait()

    def apply(data, firsts, j, dims):
        high = data.astype(jnp.bfloat16).astype(jnp.float32)
        low = data - high
        total = None
        for a in range(NAPER):
            r0 = firsts[a]
            slab_high = high[r0:r0 + rows].reshape(flat, 2 * TB)
            slab_low = low[r0:r0 + rows].reshape(flat, 2 * TB)
            stacked = jnp.concatenate([slab_high, slab_low], axis=0).astype(jnp.bfloat16)
            main = lax.dot_general(stacked, bh[a, j], dims, preferred_element_type=jnp.float32)
            rest = lax.dot_general(
                slab_high.astype(jnp.bfloat16), bl[a, j], dims, preferred_element_type=jnp.float32
            )
            term = main[:flat] + (main[flat:] + rest)
            total = term if total is None else total + term
        return total

    def migrate(values, u, arrivals):
        carried = None
        for j in range(tiles):
            cols = slice(j * TB, (j + 1) * TB)
            for message in arrivals.get(j, ()):
                message.received()
            data = jnp.concatenate([values[0, :, :, cols], values[1, :, :, cols]], axis=2)
            part = apply(data, [2 * APER - a for a in range(NAPER)], j, (((1,), (1,)), ((), ())))
            head = part[:, :TB] if carried is None else part[:, :TB] + carried
            ext[u, APER:APER + rows, :, cols] = head.reshape(rows, xl, TB)
            carried = part[:, TB:]
        ext[u, APER:APER + rows, :, window:window + TB] = carried.reshape(rows, xl, TB)

    def demigrate(u, store):
        for j in range(tiles):
            data = img[u, :, :, j * TB:(j + 2) * TB]
            part = apply(data, list(range(NAPER)), j, (((1,), (0,)), ((), ())))
            store(j, part.reshape(rows, xl, 2 * TB))

    def swap_edges(u):
        messages = []
        for source, target, di in ((first_rows, hi_halo, -1), (last_rows, lo_halo, 1)):
            messages.append(neighbour(ext.at[u, source], ext.at[u, target], di, 0))
            messages.append(neighbour(
                ext.at[u, source, :, pl.ds(0, TB)], next_strip.at[u, target], di, -1))
            messages.append(neighbour(
                ext.at[u, source, :, pl.ds(window, TB)], prev_strip.at[u, target], di, 1))
        messages.append(neighbour(
            ext.at[u, body, :, pl.ds(0, TB)], next_strip.at[u, body], 0, -1))
        messages.append(neighbour(
            ext.at[u, body, :, pl.ds(window, TB)], prev_strip.at[u, body], 0, 1))
        return messages

    def whole(u):
        earlier = ext[u, :, :, :TB] + prev_strip[u]
        earlier = jnp.where(t == 0, jnp.zeros_like(earlier), earlier)
        return [
            (slice(0, TB), earlier),
            (slice(TB, window), ext[u, :, :, TB:window]),
            (slice(window, window + TB), ext[u, :, :, window:] + next_strip[u]),
        ]

    def tile_sum(value):
        value = value.reshape(-1, xl, window)
        folded = sum(value[:, :, c * TB:(c + 1) * TB] for c in range(tiles))
        return jnp.sum(folded, axis=0)

    def start_total(turn, parts):
        for n, part in enumerate(parts):
            sa[turn, m, n:n + 1] = jnp.sum(part, axis=0, keepdims=True)
        sa[turn, m, len(parts):] = jnp.zeros((K - len(parts), TB), jnp.float32)
        messages = []
        for d in range(1, plane):
            peer = lax.rem(m + d, plane)
            messages.append(send(
                sa.at[turn, m], sa.at[turn, m], (lax.div(peer, n_tm), i, lax.rem(peer, n_tm))))
        return messages

    def next_total(turn, messages):
        for message in messages:
            message.received()
        sb[turn, i] = sum(sa[turn, s] for s in range(plane))
        return [
            send(sb.at[turn, i], sb.at[turn, i], (o, lax.rem(i + d, n_in), t))
            for d in range(1, n_in)
        ]

    def end_total(turn, messages):
        for message in messages:
            message.received()
        total = sum(sb[turn, s] for s in range(n_in))
        total = jnp.sum(total, axis=1, keepdims=True)
        return [total[n:n + 1] for n in range(3)]

    def own_image(u):
        return img[u, APER:APER + rows, :, LAG:]

    migrate(vt, 0, entry)
    for message in swap_edges(0):
        message.received()
    for cols, value in whole(0):
        img[0, :, :, cols] = value
    mg0_msg = send(img.at[0, body, :, pl.ds(LAG, window)], mg.at[0], (other, i, t))

    def store_p0(j, part):
        for slot in range(2):
            p0[slot, APER:APER + rows, :, j * TB:(j + 1) * TB] = part[:, :, slot * TB:(slot + 1) * TB]

        cols = pl.ds(j * TB, TB)
        halo[j] = [
            neighbour(p0.at[:, first_rows, :, cols], p0.at[:, hi_halo, :, cols], -1, 0),
            neighbour(p0.at[:, last_rows, :, cols], p0.at[:, lo_halo, :, cols], 1, 0),
        ]

    halo = {}
    demigrate(0, store_p0)
    own_p0 = p0[:, APER:APER + rows]
    messages = start_total(0, [tile_sum(own_image(0) * own_image(0)), tile_sum(own_p0 * own_p0)])
    px0_msg = send(p0.at[1, body], px.at[0], (other, i, t))
    migrate(p0, 1, halo)
    edges = swap_edges(1)
    messages = next_total(0, messages)
    for message in edges:
        message.received()
    gnorm, curvature, _ = end_total(0, messages)
    step0 = gnorm / curvature
    for cols, value in whole(1):
        img[1, :, :, cols] = img[0, :, :, cols] - step0[None] * value
    mg1_msg = send(img.at[1, body, :, pl.ds(LAG, window)], mg.at[1], (other, i, t))

    def store_p1(j, part):
        for slot in range(2):
            p1[slot, :, :, j * TB:(j + 1) * TB] = part[:, :, slot * TB:(slot + 1) * TB]

    demigrate(1, store_p1)
    own_p0 = p0[:, APER:APER + rows]
    own_p1 = p1[...]
    messages = start_total(1, [
        tile_sum(own_image(1) * own_image(1)), tile_sum(own_p1 * own_p1), tile_sum(own_p1 * own_p0)])
    px1_msg = send(p1.at[1], px.at[1], (other, i, t))
    messages = next_total(1, messages)
    gnew, square, cross = end_total(1, messages)
    beta = gnew / gnorm
    step1 = gnew / (square + 2.0 * beta * cross + beta * beta * curvature)
    step0, step1, beta = step0[None], step1[None], beta[None]

    def image_of(g0, g1):
        return step0 * g0 + step1 * (g1 + beta * g0)

    def residual_of(r0, a0, a1):
        return r0 - step0 * a0 - step1 * (a1 + beta * a0)

    mig_ref[:, own_x, :] = image_of(own_image(0), own_image(1))
    res_ref[0, :, own_x, :] = residual_of(vt[0, APER:APER + rows], p0[0, APER:APER + rows], p1[0])
    spare_copy.wait()
    for message in (mg0_msg, px0_msg, mg1_msg, px1_msg):
        message.received()
    mig_ref[:, other_x, :] = image_of(mg[0], mg[1])
    res_ref[0, :, other_x, :] = residual_of(spare[...], px[0], px[1])
    for message in pending:
        message.sent()


def on_device_pair(n_in, n_tm, traces, class_of_block, band_start, band_weights):
    rows, crosslines, window = traces.shape[1:]
    xl = crosslines // 2
    wide = rows + 2 * APER
    tiles = window // TB
    messages = 96
    f32 = jnp.float32
    vmem = pl.BlockSpec(memory_space=pltpu.VMEM)
    hbm = pl.BlockSpec(memory_space=pltpu.HBM)
    return pl.pallas_call(
        functools.partial(kernel, n_in, n_tm),
        out_shape=(
            jax.ShapeDtypeStruct((rows, crosslines, window), f32),
            jax.ShapeDtypeStruct((1, rows, crosslines, window), f32),
        ),
        in_specs=[pl.BlockSpec(memory_space=pltpu.SMEM), hbm, hbm, hbm],
        out_specs=(vmem, vmem),
        scratch_shapes=[
            pltpu.VMEM((2, wide, xl, window), f32),
            pltpu.VMEM((2, wide, xl, window), f32),
            pltpu.VMEM((2, rows, xl, window), f32),
            pltpu.VMEM((2, wide, xl, window + LAG), f32),
            pltpu.VMEM((2, wide, xl, TB), f32),
            pltpu.VMEM((2, wide, xl, TB), f32),
            pltpu.VMEM((2, wide, xl, window + LAG), f32),
            pltpu.VMEM((NAPER, tiles, 2 * TB, 2 * TB), jnp.bfloat16),
            pltpu.VMEM((NAPER, tiles, 2 * TB, 2 * TB), jnp.bfloat16),
            pltpu.VMEM((2, K, TB), jnp.int32),
            pltpu.VMEM((2, 2 * n_tm, K, TB), f32),
            pltpu.VMEM((2, n_in, K, TB), f32),
            pltpu.VMEM((2, rows, xl, window), f32),
            pltpu.VMEM((2, rows, xl, window), f32),
            pltpu.VMEM((NAPER,) + band_start.shape[:1] + (window,), jnp.int32),
            pltpu.VMEM(band_weights.shape, f32),
            pltpu.VMEM((rows, xl, window), f32),
            pltpu.SemaphoreType.DMA((4,)),
            pltpu.SemaphoreType.DMA((messages,)),
            pltpu.SemaphoreType.DMA((messages,)),
        ],
        compiler_params=pltpu.CompilerParams(
            collective_id=0, has_side_effects=True, vmem_limit_bytes=60 * 1024 * 1024
        ),
    )(class_of_block, traces, band_start.transpose(1, 0, 2), band_weights)


def solution(mesh):
    placed = (
        P("offset", "inline", None, "tm"),
        P("offset"),
        P(None, None, "tm"),
        P(None, None, None, "tm"),
    )
    if mesh.shape["offset"] == 2:
        body = functools.partial(on_device_pair, mesh.shape["inline"], mesh.shape["tm"])
    else:
        body = on_device_general
    return jax.shard_map(
        body,
        mesh=mesh,
        in_specs=placed,
        out_specs=(P("inline", None, "tm"), P("offset", "inline", None, "tm")),
        check_vma=False,
    )
```

```python
import functools

import jax
import jax.numpy as jnp
from jax import lax
from jax.experimental import pallas as pl
from jax.experimental.pallas import tpu as pltpu
from jax.sharding import PartitionSpec as P

K = 8
LAG = 128
APER = 2
ITERS = 2


def with_halo(block, sides, width):
    for axis, dim in sides:
        count = lax.axis_size(axis)
        forward = [(i, i + 1) for i in range(count - 1)]
        backward = [(target, source) for source, target in forward]
        low = lax.ppermute(
            lax.slice_in_dim(block, block.shape[dim] - width, None, axis=dim), axis, forward
        )
        high = lax.ppermute(lax.slice_in_dim(block, 0, width, axis=dim), axis, backward)
        block = jnp.concatenate([low, block, high], axis=dim)
    return block


def shifted(shard, axis, by):
    count = lax.axis_size(axis)
    pairs = [(i, i + by) for i in range(count) if 0 <= i + by < count]
    return lax.ppermute(shard, axis, pairs)


def widen_inline(field):
    return with_halo(field, (("inline", 1),), APER)


def totalled(value):
    return lax.psum(value, ("offset", "inline", "tm"))


def on_device_general(traces, class_of_block, band_start, band_weights):
    own_class = class_of_block[0]
    weights = lax.dynamic_index_in_dim(band_weights, own_class, 0, keepdims=False)
    starts = lax.dynamic_index_in_dim(band_start, own_class, 0, keepdims=False)
    inlines = traces.shape[1]
    crosslines = traces.shape[2]
    window = traces.shape[3]
    flat_rows = inlines * crosslines
    sample_rows = jnp.arange(window, dtype=jnp.int32)[:, None]
    sample_cols = jnp.arange(window + LAG, dtype=jnp.int32)[None, :]
    band_list = []
    for aper_index in range(2 * APER + 1):
        band_matrix = jnp.zeros((window, window + LAG), jnp.float32)
        for tap_index in range(K):
            target = sample_rows - starts[aper_index][:, None] - tap_index + LAG
            band_matrix = band_matrix + jnp.where(
                sample_cols == target, weights[aper_index, tap_index][:, None], 0.0
            )
        band_list.append(band_matrix)

    def migrate_block(values):
        widened = widen_inline(values)[0]
        result_sum = jnp.zeros((flat_rows, window + LAG), jnp.float32)
        for aper_index in range(2 * APER + 1):
            first = 2 * APER - aper_index
            slab_rows = widened[first : first + inlines].reshape(flat_rows, window)
            result_sum = result_sum + jnp.dot(
                slab_rows,
                band_list[aper_index],
                precision=lax.Precision.HIGHEST,
                preferred_element_type=jnp.float32,
            )
        result_sum = result_sum.reshape(inlines, crosslines, window + LAG)
        later_part = shifted(result_sum[:, :, :LAG], "tm", -1)
        own_part = result_sum[:, :, LAG:]
        return own_part.at[:, :, window - LAG :].add(later_part)

    def migrate(values):
        partial_image = migrate_block(values)
        gradient = lax.psum(partial_image, "offset")
        grad_norm = totalled(jnp.sum(gradient * gradient)) / lax.axis_size("offset")
        return (gradient, grad_norm)

    migrated = jnp.zeros((inlines, crosslines, window), jnp.float32)
    residual = traces
    gradient, grad_norm = migrate(residual)
    direction = gradient
    for iteration in range(ITERS):
        demigrate_widened = widen_inline(direction[None])[0]
        earlier = shifted(demigrate_widened[:, :, window - LAG :], "tm", 1)
        full_block = jnp.concatenate([earlier, demigrate_widened], axis=2)
        demigrate_result_sum = jnp.zeros((flat_rows, window), jnp.float32)
        for demigrate_aper_index in range(2 * APER + 1):
            demigrate_slab_rows = full_block[
                demigrate_aper_index : demigrate_aper_index + inlines
            ].reshape(flat_rows, window + LAG)
            demigrate_result_sum = demigrate_result_sum + lax.dot_general(
                demigrate_slab_rows,
                band_list[demigrate_aper_index],
                (((1,), (1,)), ((), ())),
                precision=lax.Precision.HIGHEST,
                preferred_element_type=jnp.float32,
            )
        projected = demigrate_result_sum.reshape(1, inlines, crosslines, window)
        curvature = totalled(jnp.sum(projected * projected))
        step_size = grad_norm / curvature
        migrated = migrated + step_size * direction
        residual = residual - step_size * projected
        if iteration + 1 < ITERS:
            gradient, grad_new = migrate(residual)
            direction = gradient + grad_new / grad_norm * direction
            grad_norm = grad_new
    return (migrated, residual)


TB = 128
MESH = pl.DeviceIdType.MESH
NAPER = 2 * APER + 1


def kernel(
    n_in, n_tm,
    cls_ref, tr_ref, st_hbm, w_hbm, mig_ref, res_ref,
    vt, p0, p1, ext, prev_strip, next_strip, img, bh, bl, cl, sa, sb, mg, px,
    st_ref, w_ref, spare, local_sem, send_sem, recv_sem,
):
    o = lax.axis_index("offset")
    i = lax.axis_index("inline")
    t = lax.axis_index("tm")
    other = 1 - o
    rows, window = tr_ref.shape[1], tr_ref.shape[3]
    xl = tr_ref.shape[2] // 2
    tiles = window // TB
    flat = rows * xl
    own_x = pl.ds(pl.multiple_of(o * xl, xl), xl)
    other_x = pl.ds(pl.multiple_of(other * xl, xl), xl)
    plane = 2 * n_tm
    m = o * n_tm + t

    start_copy = pltpu.make_async_copy(st_hbm, st_ref, local_sem.at[0])
    weight_copy = pltpu.make_async_copy(w_hbm, w_ref, local_sem.at[1])
    own_copy = pltpu.make_async_copy(tr_ref.at[0, :, own_x], vt.at[0, pl.ds(APER, rows)], local_sem.at[2])
    spare_copy = pltpu.make_async_copy(tr_ref.at[0, :, other_x], spare, local_sem.at[3])
    local_copies = (start_copy, weight_copy, own_copy, spare_copy)

    barrier = pltpu.get_barrier_semaphore()
    greeted = []
    for d in range(1, plane):
        peer = lax.rem(m + d, plane)
        greeted.append((lax.div(peer, n_tm), i, lax.rem(peer, n_tm)))
    for d in range(1, n_in):
        greeted.append((o, lax.rem(i + d, n_in), t))
    for di in sorted({1 % n_in, n_in - 1} - {0}):
        greeted.append((other, lax.rem(i + di, n_in), t))
        for dt in sorted({1 % n_tm, n_tm - 1} - {0}):
            greeted.append((o, lax.rem(i + di, n_in), lax.rem(t + dt, n_tm)))
    for device in greeted:
        pl.semaphore_signal(barrier, inc=1, device_id=device, device_id_type=MESH)
    for copy in local_copies:
        copy.start()
    pl.semaphore_wait(barrier, len(greeted))

    used = [0]

    def both(first, second):
        if first is None:
            return second
        if second is None:
            return first
        return jnp.logical_and(first, second)

    def inside(index, step, count):
        if step == 0:
            return None
        if step > 0:
            return index + step < count
        return index + step >= 0

    def guarded(condition, action):
        if condition is None:
            action()
        else:
            pl.when(condition)(action)

    class Message:
        def __init__(self, src, dst, device, can_send=None, can_receive=None):
            number = used[0]
            used[0] += 1
            self.copy = pltpu.make_async_remote_copy(
                src_ref=src, dst_ref=dst,
                send_sem=send_sem.at[number], recv_sem=recv_sem.at[number],
                device_id=device, device_id_type=MESH,
            )
            self.can_send, self.can_receive = can_send, can_receive
            guarded(can_send, self.copy.start)

        def received(self):
            guarded(self.can_receive, self.copy.wait_recv)

        def sent(self):
            guarded(self.can_send, self.copy.wait_send)

    pending = []

    def send(*args):
        message = Message(*args)
        pending.append(message)
        return message

    def neighbour(src, dst, di, dt, do=0):
        return send(
            src, dst, (o if do == 0 else other, i + di, t + dt),
            both(inside(i, di, n_in), inside(t, dt, n_tm)),
            both(inside(i, -di, n_in), inside(t, -dt, n_tm)),
        )

    lo_halo, hi_halo = pl.ds(0, APER), pl.ds(APER + rows, APER)
    body = pl.ds(APER, rows)
    first_rows, last_rows = pl.ds(APER, APER), pl.ds(rows, APER)

    cl[0] = jnp.full(cl.shape[1:], cls_ref[0], jnp.int32)
    class_msg = send(cl.at[0], cl.at[1], (other, i, t))
    entry = {}
    part = max(1, tiles // 2) * TB
    for begin in range(0, window, part):
        piece = pl.ds(begin, min(part, window - begin))
        arriving = entry[begin // TB] = []
        for slot, xs in ((1, other_x), (0, own_x)):
            arriving.append(neighbour(
                tr_ref.at[0, pl.ds(0, APER), xs, piece], vt.at[slot, hi_halo, :, piece], -1, 0, slot))
            arriving.append(neighbour(
                tr_ref.at[0, pl.ds(rows - APER, APER), xs, piece],
                vt.at[slot, lo_halo, :, piece], 1, 0, slot))
        arriving.append(send(
            tr_ref.at[0, :, other_x, piece], vt.at[1, body, :, piece], (other, i, t)))

    @pl.when(i == 0)
    def _():
        vt[:, 0:APER] = jnp.zeros_like(vt[:, 0:APER])
        p0[:, 0:APER] = jnp.zeros_like(p0[:, 0:APER])
        for u in range(2):
            ext[u, 0:APER] = jnp.zeros_like(ext[u, 0:APER])
            prev_strip[u, 0:APER] = jnp.zeros_like(prev_strip[u, 0:APER])
            next_strip[u, 0:APER] = jnp.zeros_like(next_strip[u, 0:APER])

    @pl.when(i == n_in - 1)
    def _():
        top = slice(APER + rows, 2 * APER + rows)
        vt[:, top] = jnp.zeros_like(vt[:, top])
        p0[:, top] = jnp.zeros_like(p0[:, top])
        for u in range(2):
            ext[u, top] = jnp.zeros_like(ext[u, top])
            prev_strip[u, top] = jnp.zeros_like(prev_strip[u, top])
            next_strip[u, top] = jnp.zeros_like(next_strip[u, top])

    @pl.when(jnp.logical_and(t == 0, i >= 0))
    def _():
        prev_strip[:, APER:APER + rows] = jnp.zeros_like(prev_strip[:, APER:APER + rows])

        @pl.when(i > 0)
        def _():
            prev_strip[:, 0:APER] = jnp.zeros_like(prev_strip[:, 0:APER])

        @pl.when(i < n_in - 1)
        def _():
            top = slice(APER + rows, 2 * APER + rows)
            prev_strip[:, top] = jnp.zeros_like(prev_strip[:, top])

    @pl.when(t == n_tm - 1)
    def _():
        next_strip[:, APER:APER + rows] = jnp.zeros_like(next_strip[:, APER:APER + rows])

        @pl.when(i > 0)
        def _():
            next_strip[:, 0:APER] = jnp.zeros_like(next_strip[:, 0:APER])

        @pl.when(i < n_in - 1)
        def _():
            top = slice(APER + rows, 2 * APER + rows)
            next_strip[:, top] = jnp.zeros_like(next_strip[:, top])

    sub = lax.broadcasted_iota(jnp.int32, (K, TB), 0)
    lane = lax.broadcasted_iota(jnp.int32, (K, TB), 1)
    groups = lax.broadcasted_iota(jnp.int32, (2 * TB // K, K, TB), 0)

    def build(slot):
        masks = [cl[slot] == c for c in range(st_ref.shape[1])]

        def one(j, carry):
            cols = pl.ds(pl.multiple_of(j * TB, TB), TB)
            for a in range(NAPER):
                start = jnp.zeros((K, TB), jnp.int32)
                taps = jnp.zeros((K, TB), jnp.float32)
                for c, mask in enumerate(masks):
                    row = jnp.broadcast_to(st_ref[a, c:c + 1, cols], (K, TB))
                    start = jnp.where(mask, row, start)
                    taps = jnp.where(mask, w_ref[c, a, :, cols], taps)
                reach = lane + LAG - start - sub
                group = lax.shift_right_logical(reach, 3)
                tap = jnp.bitwise_and(reach, K - 1)
                turned = jnp.zeros((K, TB), jnp.float32)
                for k in range(K):
                    turned = jnp.where(tap == k, jnp.broadcast_to(taps[k:k + 1], (K, TB)), turned)
                high = turned.astype(jnp.bfloat16).astype(jnp.float32)
                low = turned - high
                hit = groups == group[None]
                place = slice(slot * TB, (slot + 1) * TB)
                bh[a, j, :, place] = jnp.where(hit, high[None], 0.0).reshape(2 * TB, TB).astype(jnp.bfloat16)
                bl[a, j, :, place] = jnp.where(hit, low[None], 0.0).reshape(2 * TB, TB).astype(jnp.bfloat16)
            return carry

        lax.fori_loop(0, tiles, one, 0)

    start_copy.wait()
    weight_copy.wait()
    build(0)
    class_msg.received()
    build(1)
    own_copy.wait()

    def apply(data, firsts, j, dims):
        high = data.astype(jnp.bfloat16).astype(jnp.float32)
        low = data - high
        total = None
        for a in range(NAPER):
            r0 = firsts[a]
            slab_high = high[r0:r0 + rows].reshape(flat, 2 * TB)
            slab_low = low[r0:r0 + rows].reshape(flat, 2 * TB)
            stacked = jnp.concatenate([slab_high, slab_low], axis=0).astype(jnp.bfloat16)
            main = lax.dot_general(stacked, bh[a, j], dims, preferred_element_type=jnp.float32)
            rest = lax.dot_general(
                slab_high.astype(jnp.bfloat16), bl[a, j], dims, preferred_element_type=jnp.float32
            )
            term = main[:flat] + (main[flat:] + rest)
            total = term if total is None else total + term
        return total

    def migrate(values, u, arrivals):
        carried = None
        for j in range(tiles):
            cols = slice(j * TB, (j + 1) * TB)
            for message in arrivals.get(j, ()):
                message.received()
            data = jnp.concatenate([values[0, :, :, cols], values[1, :, :, cols]], axis=2)
            part = apply(data, [2 * APER - a for a in range(NAPER)], j, (((1,), (1,)), ((), ())))
            head = part[:, :TB] if carried is None else part[:, :TB] + carried
            ext[u, APER:APER + rows, :, cols] = head.reshape(rows, xl, TB)
            carried = part[:, TB:]
        ext[u, APER:APER + rows, :, window:window + TB] = carried.reshape(rows, xl, TB)

    def demigrate(u, store):
        for j in range(tiles):
            data = img[u, :, :, j * TB:(j + 2) * TB]
            part = apply(data, list(range(NAPER)), j, (((1,), (0,)), ((), ())))
            store(j, part.reshape(rows, xl, 2 * TB))

    def swap_edges(u):
        messages = []
        for source, target, di in ((first_rows, hi_halo, -1), (last_rows, lo_halo, 1)):
            messages.append(neighbour(ext.at[u, source], ext.at[u, target], di, 0))
            messages.append(neighbour(
                ext.at[u, source, :, pl.ds(0, TB)], next_strip.at[u, target], di, -1))
            messages.append(neighbour(
                ext.at[u, source, :, pl.ds(window, TB)], prev_strip.at[u, target], di, 1))
        messages.append(neighbour(
            ext.at[u, body, :, pl.ds(0, TB)], next_strip.at[u, body], 0, -1))
        messages.append(neighbour(
            ext.at[u, body, :, pl.ds(window, TB)], prev_strip.at[u, body], 0, 1))
        return messages

    def whole(u):
        earlier = ext[u, :, :, :TB] + prev_strip[u]
        earlier = jnp.where(t == 0, jnp.zeros_like(earlier), earlier)
        return [
            (slice(0, TB), earlier),
            (slice(TB, window), ext[u, :, :, TB:window]),
            (slice(window, window + TB), ext[u, :, :, window:] + next_strip[u]),
        ]

    def tile_sum(value):
        value = value.reshape(-1, xl, window)
        folded = sum(value[:, :, c * TB:(c + 1) * TB] for c in range(tiles))
        return jnp.sum(folded, axis=0)

    def start_total(turn, parts):
        for n, part in enumerate(parts):
            sa[turn, m, n:n + 1] = jnp.sum(part, axis=0, keepdims=True)
        sa[turn, m, len(parts):] = jnp.zeros((K - len(parts), TB), jnp.float32)
        messages = []
        for d in range(1, plane):
            peer = lax.rem(m + d, plane)
            messages.append(send(
                sa.at[turn, m], sa.at[turn, m], (lax.div(peer, n_tm), i, lax.rem(peer, n_tm))))
        return messages

    def next_total(turn, messages):
        for message in messages:
            message.received()
        sb[turn, i] = sum(sa[turn, s] for s in range(plane))
        return [
            send(sb.at[turn, i], sb.at[turn, i], (o, lax.rem(i + d, n_in), t))
            for d in range(1, n_in)
        ]

    def end_total(turn, messages):
        for message in messages:
            message.received()
        total = sum(sb[turn, s] for s in range(n_in))
        total = jnp.sum(total, axis=1, keepdims=True)
        return [total[n:n + 1] for n in range(3)]

    def own_image(u):
        return img[u, APER:APER + rows, :, LAG:]

    migrate(vt, 0, entry)
    for message in swap_edges(0):
        message.received()
    for cols, value in whole(0):
        img[0, :, :, cols] = value
    mg0_msg = send(img.at[0, body, :, pl.ds(LAG, window)], mg.at[0], (other, i, t))

    def store_p0(j, part):
        for slot in range(2):
            p0[slot, APER:APER + rows, :, j * TB:(j + 1) * TB] = part[:, :, slot * TB:(slot + 1) * TB]

        cols = pl.ds(j * TB, TB)
        halo[j] = [
            neighbour(p0.at[:, first_rows, :, cols], p0.at[:, hi_halo, :, cols], -1, 0),
            neighbour(p0.at[:, last_rows, :, cols], p0.at[:, lo_halo, :, cols], 1, 0),
        ]

    halo = {}
    demigrate(0, store_p0)
    own_p0 = p0[:, APER:APER + rows]
    messages = start_total(0, [tile_sum(own_image(0) * own_image(0)), tile_sum(own_p0 * own_p0)])
    px0_msg = send(p0.at[1, body], px.at[0], (other, i, t))
    migrate(p0, 1, halo)
    edges = swap_edges(1)
    messages = next_total(0, messages)
    for message in edges:
        message.received()
    gnorm, curvature, _ = end_total(0, messages)
    step0 = gnorm / curvature
    for cols, value in whole(1):
        img[1, :, :, cols] = img[0, :, :, cols] - step0[None] * value

    def store_p1(j, part):
        for slot in range(2):
            p1[slot, :, :, j * TB:(j + 1) * TB] = part[:, :, slot * TB:(slot + 1) * TB]

    demigrate(1, store_p1)
    own_p0 = p0[:, APER:APER + rows]
    own_p1 = p1[...]
    messages = start_total(1, [
        tile_sum(own_image(1) * own_image(1)), tile_sum(own_p1 * own_p1), tile_sum(own_p1 * own_p0)])
    mg1_msg = send(img.at[1, body, :, pl.ds(LAG, window)], mg.at[1], (other, i, t))
    px1_msg = send(p1.at[1], px.at[1], (other, i, t))
    messages = next_total(1, messages)
    gnew, square, cross = end_total(1, messages)
    beta = gnew / gnorm
    step1 = gnew / (square + 2.0 * beta * cross + beta * beta * curvature)
    step0, step1, beta = step0[None], step1[None], beta[None]

    def image_of(g0, g1):
        return step0 * g0 + step1 * (g1 + beta * g0)

    def residual_of(r0, a0, a1):
        return r0 - step0 * a0 - step1 * (a1 + beta * a0)

    mig_ref[:, own_x, :] = image_of(own_image(0), own_image(1))
    res_ref[0, :, own_x, :] = residual_of(vt[0, APER:APER + rows], p0[0, APER:APER + rows], p1[0])
    spare_copy.wait()
    for message in (mg0_msg, px0_msg, mg1_msg, px1_msg):
        message.received()
    mig_ref[:, other_x, :] = image_of(mg[0], mg[1])
    res_ref[0, :, other_x, :] = residual_of(spare[...], px[0], px[1])
    for message in pending:
        message.sent()


def on_device_pair(n_in, n_tm, traces, class_of_block, band_start, band_weights):
    rows, crosslines, window = traces.shape[1:]
    xl = crosslines // 2
    wide = rows + 2 * APER
    tiles = window // TB
    messages = 96
    f32 = jnp.float32
    vmem = pl.BlockSpec(memory_space=pltpu.VMEM)
    hbm = pl.BlockSpec(memory_space=pltpu.HBM)
    return pl.pallas_call(
        functools.partial(kernel, n_in, n_tm),
        out_shape=(
            jax.ShapeDtypeStruct((rows, crosslines, window), f32),
            jax.ShapeDtypeStruct((1, rows, crosslines, window), f32),
        ),
        in_specs=[pl.BlockSpec(memory_space=pltpu.SMEM), hbm, hbm, hbm],
        out_specs=(vmem, vmem),
        scratch_shapes=[
            pltpu.VMEM((2, wide, xl, window), f32),
            pltpu.VMEM((2, wide, xl, window), f32),
            pltpu.VMEM((2, rows, xl, window), f32),
            pltpu.VMEM((2, wide, xl, window + LAG), f32),
            pltpu.VMEM((2, wide, xl, TB), f32),
            pltpu.VMEM((2, wide, xl, TB), f32),
            pltpu.VMEM((2, wide, xl, window + LAG), f32),
            pltpu.VMEM((NAPER, tiles, 2 * TB, 2 * TB), jnp.bfloat16),
            pltpu.VMEM((NAPER, tiles, 2 * TB, 2 * TB), jnp.bfloat16),
            pltpu.VMEM((2, K, TB), jnp.int32),
            pltpu.VMEM((2, 2 * n_tm, K, TB), f32),
            pltpu.VMEM((2, n_in, K, TB), f32),
            pltpu.VMEM((2, rows, xl, window), f32),
            pltpu.VMEM((2, rows, xl, window), f32),
            pltpu.VMEM((NAPER,) + band_start.shape[:1] + (window,), jnp.int32),
            pltpu.VMEM(band_weights.shape, f32),
            pltpu.VMEM((rows, xl, window), f32),
            pltpu.SemaphoreType.DMA((4,)),
            pltpu.SemaphoreType.DMA((messages,)),
            pltpu.SemaphoreType.DMA((messages,)),
        ],
        compiler_params=pltpu.CompilerParams(
            collective_id=0, has_side_effects=True, vmem_limit_bytes=60 * 1024 * 1024
        ),
    )(class_of_block, traces, band_start.transpose(1, 0, 2), band_weights)


def solution(mesh):
    placed = (
        P("offset", "inline", None, "tm"),
        P("offset"),
        P(None, None, "tm"),
        P(None, None, None, "tm"),
    )
    if mesh.shape["offset"] == 2:
        body = functools.partial(on_device_pair, mesh.shape["inline"], mesh.shape["tm"])
    else:
        body = on_device_general
    return jax.shard_map(
        body,
        mesh=mesh,
        in_specs=placed,
        out_specs=(P("inline", None, "tm"), P("offset", "inline", None, "tm")),
        check_vma=False,
    )
```
